128 devices in a mesh: grp: 4 (over z), shard: 32 (over y, x, core).
Axes of the slice: x: 4, y: 4, z: 4, core: 2. Of those that a mesh axis runs over, the one named last changes fastest.
Arguments:
- context: bfloat16 [196608, 2048], P(('grp', 'shard')), may hold values from -24 to 24
- out_grad: bfloat16 [196608, 4096], P(('grp', 'shard')), may hold values from -0.013671875 to 0.013671875
- old_master: float32 [32, 4, 131072], P('shard', 'grp'), may hold values from -0.125 to 0.125
- old_mom1: float32 [32, 4, 131072], P('shard', 'grp'), may hold values from -6 to 6
- old_mom2: float32 [32, 4, 131072], P('shard', 'grp'), may hold values from 0.05 to 1
- old_lengths: int32 [32, 4], P('shard'), may hold values from 1 to 131072, 262144 in all within a row
Outputs:
- new_master: float32 [32, 64, 4096], P('shard', 'grp')
- new_mom1: float32 [32, 64, 4096], P('shard', 'grp')
- new_mom2: float32 [32, 64, 4096], P('shard', 'grp')
- weights_bf16: bfloat16 [32, 64, 4096], P('shard')
The draws below stay inside these ranges and needn't reach their ends.
Inputs may be any that keep to these rules, and one draw needn't show every extreme that they name: `old_lengths`: each row sums to 262144, and its largest entry is exactly 131072.
All inputs are finite; a program needn't handle non-finite values.
Results may differ from the reference program's by a relative error of at most 0.0055.
Values may be sent and summed in bfloat16 or wider, within the bound.
No kernel may reach another device: no remote copies, remote signals or barrier semaphores. Data moves between devices by JAX's collectives and lax.ppermute only.
A program may use at most 256 MiB of HBM per device.

```python
import math
import jax
import jax.numpy as jnp
import numpy as np
from jax import lax

D = 4096
HD = 2048
TOKENS = 196608
ROWS_OWN = 16
BLOCK = 65536
CAP = 131072
N_GRP = 4
N_SHARD = 32


def raised(entries, rng, source, target, shards_of, factor):
    owner, partner = [(jnp.arange(entries.shape[axis_at]) // (entries.shape[axis_at] // shards_of)).reshape([-1 if axis == axis_at else 1 for axis in range(entries.ndim)]) for axis_at in (source, target)]
    chosen = jax.random.permutation(rng, shards_of)[partner]
    strong = (owner == chosen) | (owner == (partner + shards_of // 2) % shards_of)
    return jnp.where(strong, factor * entries, entries)


def shard_levels(own_key, dims, cuts, smallest, largest):
    def one(dim, shards_of):
        heights = jax.random.uniform(jax.random.fold_in(jax.random.fold_in(own_key, 6), dim), (shards_of,), jnp.float32, smallest / len(cuts), largest / len(cuts))
        return jnp.repeat(jnp.exp(heights), dims[dim] // shards_of).reshape((-1,) + (1,) * (len(dims) - dim - 1))

    gain = one(*cuts[0])
    for cut in cuts[1:]:
        gain = gain * one(*cut)
    return gain


def length_profile(number_of, total, bound, skew):
    loads = [(1 << 20) // math.isqrt(standing ** skew) + 1 for standing in range(2, number_of + 1)]
    rest, given = total - bound - (number_of - 1), [1] * (number_of - 1)
    while rest > 0:
        movable = [i for i in range(number_of - 1) if given[i] < bound]
        mass, remaining = sum([loads[i] for i in movable]), rest
        for i in movable:
            more = min(bound - given[i], max(1, remaining * loads[i] // mass), rest)
            given[i] = given[i] + more
            rest = rest - more
    return np.array([bound] + given)


def uneven(own_key, count, total, bound, lean):
    if count == 2:
        one = jax.random.randint(own_key, (), max(1, total - bound), min(bound, total - 1) + 1)
        return jnp.stack([one, total - one])
    sizes = jnp.asarray(length_profile(count, total, bound, lean), jnp.int32)
    twos = (count - 1) // 2
    donor, sink = sizes[1:1 + 2 * twos:2], sizes[2:2 + 2 * twos:2]
    margin = jnp.minimum(donor - 1, bound - sink)
    moved = jax.random.randint(jax.random.fold_in(own_key, 1), (twos,), 0, 1 << 20) % (margin + 1)
    sizes = sizes.at[1:1 + 2 * twos:2].set(donor - moved).at[2:2 + 2 * twos:2].set(sink + moved)
    return sizes[jax.random.permutation(jax.random.fold_in(own_key, 2), count)]


def noise(stream_key, shape, deviation, limit, shards=(), kind=jnp.bfloat16):
    factor_of = shard_levels(stream_key, shape, shards, -0.22, 0.18) if shards else 1.0
    result = jax.random.normal(stream_key, shape, jnp.float32) * deviation * factor_of
    return jnp.minimum(jnp.maximum(result, -limit), limit).astype(kind)


def heavy_noise(stream_key, extent, scale, bound, cuts, heavy, kind=jnp.bfloat16):
    drawn = scale * jax.random.normal(stream_key, extent, jnp.float32)
    if cuts:
        drawn = drawn * shard_levels(stream_key, extent, cuts, -0.22, 0.18)
    return jnp.clip(raised(drawn, jax.random.fold_in(stream_key, 3), *heavy), -bound, bound).astype(kind)


def setup_inputs(seed: int = 0) -> dict:
    keys = jax.random.split(jax.random.key(seed), 7)
    return {
        "context": heavy_noise(keys[0], (TOKENS, HD), 1.0, 24.0, ((0, 128),), (0, 1, 128, 5.5)),
        "out_grad": noise(keys[1], (TOKENS, D), TOKENS ** -0.5, 0.013671875, ((0, 128),)),
        "old_master": noise(keys[2], (N_SHARD, N_GRP, CAP), HD ** -0.5, 0.125, ((0, 32), (1, 4)), jnp.float32),
        "old_mom1": noise(keys[3], (N_SHARD, N_GRP, CAP), 1.0, 6.0, ((0, 32), (1, 4)), jnp.float32),
        "old_mom2": jnp.clip(jnp.exp(math.log(1.0) - 2.9957323 * jax.random.uniform(keys[4], (N_SHARD, N_GRP, CAP), jnp.float32) ** shard_levels(keys[4], (N_SHARD, N_GRP, CAP), ((0, 32), (1, 4)), -0.2, 0.2)), 0.05, 1.0),
        "old_lengths": jax.vmap(lambda own: uneven(own, N_GRP, N_GRP * BLOCK, CAP, 2))(jax.random.split(keys[5], N_SHARD)).reshape((N_SHARD, N_GRP)).astype(jnp.int32),
    }


beta_one = 0.9
beta_two = 0.95
step_size = 0.01
epsilon = 1e-08

def assemble(old_pieces, old_lengths):
    slice_total = N_GRP * BLOCK
    piece_ends = jnp.cumsum(old_lengths, axis=1).astype(jnp.int32)
    piece_starts = (piece_ends - old_lengths).astype(jnp.int32)
    position = jnp.arange(slice_total, dtype=jnp.int32)
    owner_piece = lax.optimization_barrier(jnp.sum((position[None, :, None] >= piece_ends[:, None, :]).astype(jnp.int32), axis=2)).astype(jnp.int32)
    piece_first = jnp.take_along_axis(piece_starts, owner_piece, axis=1)
    flat_index = (owner_piece * CAP + position[None, :] - piece_first).astype(jnp.int32)
    flat_pieces = old_pieces.reshape(N_SHARD, N_GRP * CAP)
    joined = jnp.take_along_axis(flat_pieces, flat_index, axis=1)
    return joined.reshape(N_SHARD, N_GRP * ROWS_OWN, D)

def reference(context, out_grad, old_master, old_mom1, old_mom2, old_lengths):
    master = assemble(old_master, old_lengths)
    first = assemble(old_mom1, old_lengths)
    second = assemble(old_mom2, old_lengths)
    gradient = jnp.dot(context.T, out_grad, preferred_element_type=jnp.float32)
    gradient = gradient.reshape(N_SHARD, N_GRP * ROWS_OWN, D)
    first_new = beta_one * first + (1.0 - beta_one) * gradient
    second_new = beta_two * second + (1.0 - beta_two) * gradient * gradient
    master_new = master - step_size * first_new / (jnp.sqrt(second_new) + epsilon)
    return (master_new, first_new, second_new, master_new.astype(jnp.bfloat16))
```

```python
import jax
import jax.numpy as jnp
from jax import lax
from jax.experimental import pallas as pl
from jax.experimental.pallas import tpu as pltpu
from jax.sharding import PartitionSpec as P

beta_one = 0.9
beta_two = 0.95
step_size = 0.01
epsilon = 1e-08

N_GRP, N_SHARD, SIDE = 4, 32, 4
ROWS = 64
CHUNKS = (2048, 2048)
f32, bf16 = jnp.float32, jnp.bfloat16


def moved(by_core):
    pairs = []
    for z in range(4):
        for y in range(4):
            for x in range(4):
                for c in range(2):
                    axis, shift = by_core[c]
                    to = {"z": z, "y": y, "x": x}
                    to[axis] = (to[axis] + shift) % 4
                    pairs.append(
                        (((z * 4 + y) * 4 + x) * 2 + c, ((to["z"] * 4 + to["y"]) * 4 + to["x"]) * 2 + c)
                    )
    return pairs


FIRST = {k: moved((("x", k), ("y", k))) for k in (1, 2, 3)}
SECOND = {k: moved((("y", k), ("x", k))) for k in (1, 2, 3)}
ALONG_Z = {k: moved((("z", k), ("z", k))) for k in (1, 2, 3)}
SWAP = [(i, i ^ 1) for i in range(128)]


def send(value, pairs):
    return lax.ppermute(value, ("grp", "shard"), pairs)


def row_table():
    shard = lax.axis_index("shard")
    c, x, y = shard % 2, (shard // 2) % 4, shard // 8

    def of(core):
        j = jnp.arange(16, dtype=jnp.int32)
        j1, j2 = j // 4, j % 4
        jx, jy = jnp.where(core == 0, j1, j2), jnp.where(core == 0, j2, j1)
        return 2 * (((y + jy) % 4) * 4 + (x + jx) % 4) + core

    return jnp.concatenate([of(c), of(1 - c)]).astype(jnp.int32)


def call(body, name, steps, in_specs, out_specs, out_shape, moved_bytes, *operands):
    return pl.pallas_call(
        body,
        grid_spec=pltpu.PrefetchScalarGridSpec(
            num_scalar_prefetch=1, grid=(steps,), in_specs=in_specs, out_specs=out_specs
        ),
        out_shape=out_shape,
        name=name,
        cost_estimate=pl.CostEstimate(flops=moved_bytes // 4, bytes_accessed=moved_bytes, transcendentals=0),
        compiler_params=pltpu.CompilerParams(vmem_limit_bytes=40 * 2**20),
    )(*operands)


def for_other_core(table, partial):
    cols = partial.shape[1]

    def body(t, p, o):
        o[0] = p[...].astype(bf16)

    return call(
        body, "for_other_core", 16,
        [pl.BlockSpec((ROWS, cols), lambda i, t: (t[16 + i], 0))],
        pl.BlockSpec((1, ROWS, cols), lambda i, t: (i, 0, 0)),
        jax.ShapeDtypeStruct((16, ROWS, cols), bf16),
        16 * ROWS * cols * 6, table, partial,
    )


def own(cols, place):
    return [
        pl.BlockSpec((ROWS, cols), lambda i, t: (t[place(i)], 0)),
        pl.BlockSpec((1, ROWS, cols), lambda i, t: (place(i), 0, 0)),
    ]


def part(cols, place):
    return pl.BlockSpec((1, ROWS, cols), lambda i, t: (place(i), 0, 0))


def first_sends(table, partial, other):
    cols = partial.shape[1]

    def body(t, p0, r0, p1, r1, plus, minus):
        plus[0] = (p0[...] + r0[0].astype(f32)).astype(bf16)
        minus[0] = (p1[...] + r1[0].astype(f32)).astype(bf16)

    return call(
        body, "first_sends", 4,
        own(cols, lambda i: jnp.where(i < 2, 8 + i, 4 + i)) + own(cols, lambda i: jnp.where(i < 2, 12 + i, 8 + i)),
        [part(cols, lambda i: i)] * 2,
        [jax.ShapeDtypeStruct((4, ROWS, cols), bf16)] * 2,
        8 * ROWS * cols * 8, table, partial, other, partial, other,
    )


def second_sends(table, partial, other, from_minus, from_plus):
    cols = partial.shape[1]

    def body(t, p0, r0, a, p1, r1, b, plus, minus):
        plus[0] = (p0[...] + r0[0].astype(f32) + a[0].astype(f32)).astype(bf16)
        minus[0] = (p1[...] + r1[0].astype(f32) + b[0].astype(f32)).astype(bf16)

    return call(
        body, "second_sends", 2,
        own(cols, lambda i: 4 + i) + [part(cols, lambda i: i)]
        + own(cols, lambda i: 14 + i) + [part(cols, lambda i: 2 + i)],
        [part(cols, lambda i: i)] * 2,
        [jax.ShapeDtypeStruct((2, ROWS, cols), bf16)] * 2,
        4 * ROWS * cols * 10, table, partial, other, from_minus, partial, other, from_plus,
    )


def first_sums(table, partial, other, from_minus, from_plus, far_minus, far_plus):
    cols = partial.shape[1]

    def body(t, p, r, a0, b0, a1, b1, keep, s1, s2, s3):
        i = pl.program_id(0)
        base = p[...] + r[0].astype(f32)

        @pl.when(i == 0)
        def _():
            keep[...] = base + a0[0].astype(f32) + b0[0].astype(f32)

        @pl.when(i == 1)
        def _():
            s1[...] = (base + a0[0].astype(f32) + b0[0].astype(f32)).astype(bf16)

        @pl.when(i == 2)
        def _():
            s2[...] = (base + a1[0].astype(f32) + b1[0].astype(f32)).astype(bf16)

        @pl.when(i == 3)
        def _():
            s3[...] = (base + a1[0].astype(f32) + b1[0].astype(f32)).astype(bf16)

    whole = pl.BlockSpec((ROWS, cols), lambda i, t: (0, 0))
    return call(
        body, "first_sums", 4,
        own(cols, lambda i: i)
        + [
            part(cols, lambda i: jnp.minimum(i, 1)),
            part(cols, lambda i: jnp.minimum(i, 1)),
            part(cols, lambda i: jnp.maximum(i, 2)),
            part(cols, lambda i: jnp.maximum(i - 2, 0)),
        ],
        [whole] * 4,
        [jax.ShapeDtypeStruct((ROWS, cols), f32)] + [jax.ShapeDtypeStruct((ROWS, cols), bf16)] * 3,
        4 * ROWS * cols * 13, table, partial, other, from_plus, far_minus, from_minus, far_plus,
    )


def windows(lengths, pieces):
    groups, my_group = N_GRP, lax.axis_index("grp")
    cap = pieces[0].shape[0] * 128
    block = N_GRP * ROWS * 4096 // N_GRP // N_GRP
    n = block // 128
    starts = jnp.cumsum(lengths) - lengths
    mine = lax.dynamic_index_in_dim(starts, my_group, keepdims=False)
    length = lax.dynamic_index_in_dim(lengths, my_group, keepdims=False)
    target = (my_group + jnp.arange(groups, dtype=jnp.int32)) % groups
    offset = target * block - mine
    row = jnp.clip(offset // 128, -n, cap // 128) + n
    scalars = jnp.concatenate([offset, row, offset % 128, length[None]]).astype(jnp.int32)

    def body(s, piece, keep, s1, s2, s3, held):
        held[pl.ds(n, cap // 128), :] = piece[0]
        lane = lax.broadcasted_iota(jnp.int32, (n, 128), 1)
        at = lax.broadcasted_iota(jnp.int32, (n, 128), 0) * 128 + lane
        for j, out in enumerate((keep, s1, s2, s3)):
            off, first, turn = s[j], s[4 + j], s[8 + j]
            low = held[pl.ds(first, n), :]
            high = held[pl.ds(first + 1, n), :]
            back = lax.rem(128 - turn, 128)
            value = jnp.where(lane < 128 - turn, pltpu.roll(low, back, 1), pltpu.roll(high, back, 1))
            inside = (at + off >= 0) & (at + off < s[12])
            out[0] = jnp.where(inside, value, 0.0).astype(out.dtype)

    spec = pl.BlockSpec((1, n, 128), lambda i, s: (i, 0, 0))
    return pl.pallas_call(
        body,
        grid_spec=pltpu.PrefetchScalarGridSpec(
            num_scalar_prefetch=1,
            grid=(3,),
            in_specs=[pl.BlockSpec((1, cap // 128, 128), lambda i, s: (i, 0, 0))],
            out_specs=[spec] * 4,
            scratch_shapes=[pltpu.VMEM((cap // 128 + 2 * n + 8, 128), f32)],
        ),
        out_shape=[jax.ShapeDtypeStruct((3, n, 128), f32)] + [jax.ShapeDtypeStruct((3, n, 128), bf16)] * 3,
        name="windows",
        cost_estimate=pl.CostEstimate(flops=10**7, bytes_accessed=4 * 10**6, transcendentals=0),
        compiler_params=pltpu.CompilerParams(vmem_limit_bytes=40 * 2**20),
    )(scalars, jnp.stack(pieces))


def local(context, out_grad, old_master, old_mom1, old_mom2, old_lengths):
    width = out_grad.shape[1]
    table = row_table()
    keep, *away = windows(old_lengths[0], [a.reshape(-1, 128) for a in (old_master, old_mom1, old_mom2)])
    arrived = [send(away[k - 1], ALONG_Z[k]) for k in (1, 2, 3)]

    gradient = []
    start = 0
    for cols in CHUNKS:
        partial = lax.dot_general(
            context, out_grad[:, start:start + cols], (((0,), (0,)), ((), ())), preferred_element_type=f32
        )
        start += cols
        other = send(for_other_core(table, partial), SWAP)
        plus, minus = first_sends(table, partial, other)
        from_minus, from_plus = send(plus, FIRST[1]), send(minus, FIRST[3])
        plus, minus = second_sends(table, partial, other, from_minus, from_plus)
        far_minus, far_plus = send(plus, FIRST[1]), send(minus, FIRST[3])
        mine, *away = first_sums(table, partial, other, from_minus, from_plus, far_minus, far_plus)
        for k in (1, 2, 3):
            mine = mine + send(away[k - 1], SECOND[k]).astype(f32)
        rows = lax.all_to_all(mine.reshape(N_GRP, ROWS // N_GRP, cols), "grp", 0, 0, tiled=True)
        gradient.append(jnp.sum(rows, axis=0))
    gradient = jnp.concatenate(gradient, axis=1)

    state = keep
    for value in arrived:
        state = state + value.astype(f32)
    state = state.reshape(3, ROWS // N_GRP, width)
    first_new = beta_one * state[1] + (1.0 - beta_one) * gradient
    second_new = beta_two * state[2] + (1.0 - beta_two) * gradient * gradient
    master_new = state[0] - step_size * first_new / (jnp.sqrt(second_new) + epsilon)
    weights = lax.all_gather(master_new.astype(bf16)[None], "grp", axis=1, tiled=True)
    return (master_new[None], first_new[None], second_new[None], weights)


def solution(mesh):
    placed = (
        P(("grp", "shard"), None),
        P(("grp", "shard"), None),
        P("shard", "grp", None),
        P("shard", "grp", None),
        P("shard", "grp", None),
        P("shard", None),
    )
    return jax.shard_map(
        local,
        mesh=mesh,
        in_specs=placed,
        out_specs=(
            P("shard", "grp", None),
            P("shard", "grp", None),
            P("shard", "grp", None),
            P("shard", None, None),
        ),
        check_vma=False,
    )
```

```python
import jax
import jax.numpy as jnp
from jax import lax
from jax.experimental import pallas as pl
from jax.experimental.pallas import tpu as pltpu
from jax.sharding import PartitionSpec as P

beta_one = 0.9
beta_two = 0.95
step_size = 0.01
epsilon = 1e-08

N_GRP = 4
ROWS = 64
CHUNKS = (2048, 2048)
TILE = 512
f32, bf16 = jnp.float32, jnp.bfloat16
AXES = ("grp", "shard")

DEVICES = [(z, y, x, c) for z in range(4) for y in range(4) for x in range(4) for c in range(2)]
SWAP = [(i, i ^ 1) for i in range(128)]


def number(z, y, x, c):
    return (((z % 4) * 4 + y % 4) * 4 + x % 4) * 2 + c


FIRST = {
    k: [(number(z, y, x, c), number(z, y + k * c, x + k * (1 - c), c)) for z, y, x, c in DEVICES] for k in (1, 2, 3)
}


def grouped(key, order):
    groups = {}
    for place in sorted(DEVICES, key=lambda place: order(*place)):
        groups.setdefault(key(*place), []).append(number(*place))
    return list(groups.values())


SECOND = grouped(lambda z, y, x, c: (c, y if c else x), lambda z, y, x, c: (y, x, z))


def row_table(shard):
    core, x, y = shard % 2, (shard // 2) % 4, shard // 8

    def of(c):
        i = jnp.arange(16, dtype=jnp.int32)
        ahead, second = i // 4, i % 4
        return 2 * jnp.where(c == 0, second * 4 + (x + ahead) % 4, (y + ahead) % 4 * 4 + second) + c

    return jnp.concatenate([of(core), of(1 - core)]).astype(jnp.int32)


def params():
    return pltpu.CompilerParams(vmem_limit_bytes=60 * 2**20)


def cost(tokens, height, cols):
    return pl.CostEstimate(
        flops=2 * tokens * height * cols // 16, bytes_accessed=(tokens + height) * cols // 8, transcendentals=0
    )


def product(left, right):
    return lax.dot_general(left, right, (((0,), (0,)), ((), ())), preferred_element_type=f32)


def first_product(table, context, out_grad, start, cols):
    tokens, height = context.shape
    half, parts = height // 2, 4
    slab = tokens // parts

    def body(t, c_hbm, g, out, mine_hbm, other_hbm, c, mine, other, arrived, left):
        step = pl.program_id(0)

        def piece(m):
            at = pl.ds(m * slab, slab)
            return pltpu.make_async_copy(c_hbm.at[at], c.at[at], arrived.at[m])

        def away():
            return [
                pltpu.make_async_copy(mine, mine_hbm, left.at[0]),
                pltpu.make_async_copy(other, other_hbm, left.at[1]),
            ]

        def choose(to, base, core):
            for m in range(parts):
                at = pl.ds(m * slab, slab)
                for k in range(8):
                    low, high = [
                        c[at, pl.ds(pl.multiple_of((t[base + 2 * k + i] >> 1) * 128, 128), 128)] for i in (0, 1)
                    ]
                    to[at, pl.ds(k * 128, 128)] = jnp.concatenate(
                        [low[:, core * 64:core * 64 + 64], high[:, core * 64:core * 64 + 64]], axis=1
                    )

        @pl.when(step == 0)
        def _():
            for m in range(parts):
                piece(m).start()
            for m in range(parts):
                piece(m).wait()

            @pl.when((t[0] & 1) == 0)
            def _():
                choose(other, 16, 1)
                choose(mine, 0, 0)

            @pl.when((t[0] & 1) == 1)
            def _():
                choose(other, 16, 0)
                choose(mine, 0, 1)

            for copy in away():
                copy.start()

        out[...] = product(other[...], g[...]).astype(bf16)

        @pl.when(step == cols // TILE - 1)
        def _():
            for copy in away():
                copy.wait()

    hbm = pl.BlockSpec(memory_space=pl.ANY)
    return pl.pallas_call(
        body,
        grid_spec=pltpu.PrefetchScalarGridSpec(
            num_scalar_prefetch=1,
            grid=(cols // TILE,),
            in_specs=[hbm, pl.BlockSpec((tokens, TILE), lambda i, t: (0, start // TILE + i))],
            out_specs=[pl.BlockSpec((half, TILE), lambda i, t: (0, i)), hbm, hbm],
            scratch_shapes=[
                pltpu.VMEM((tokens, height), bf16),
                pltpu.VMEM((tokens, half), bf16),
                pltpu.VMEM((tokens, half), bf16),
                pltpu.SemaphoreType.DMA((parts,)),
                pltpu.SemaphoreType.DMA((2,)),
            ],
        ),
        out_shape=[
            jax.ShapeDtypeStruct((half, cols), bf16),
            jax.ShapeDtypeStruct((tokens, half), bf16),
            jax.ShapeDtypeStruct((tokens, half), bf16),
        ],
        name="first_product",
        cost_estimate=cost(tokens, half, cols),
        compiler_params=params(),
    )(table, context, out_grad)


def other_product(other, out_grad, start, cols):
    tokens, half = other.shape

    def body(c, g, out):
        out[...] = product(c[...], g[...]).astype(bf16)

    return pl.pallas_call(
        body,
        grid=(cols // TILE,),
        in_specs=[
            pl.BlockSpec((tokens, half), lambda i: (0, 0), pipeline_mode=pl.Buffered(1)),
            pl.BlockSpec((tokens, TILE), lambda i: (0, start // TILE + i)),
        ],
        out_specs=pl.BlockSpec((half, TILE), lambda i: (0, i)),
        out_shape=jax.ShapeDtypeStruct((half, cols), bf16),
        name="other_product",
        cost_estimate=cost(tokens, half, cols),
        compiler_params=params(),
    )(other, out_grad)


def chip_product(mine, out_grad, received, start, cols):
    tokens, half = mine.shape
    quarter = half // 4

    def body(c, g, r, own, *away):
        total = product(c[...], g[...]) + r[...].astype(f32)
        own[...] = total[:quarter]
        for k in range(3):
            away[k][...] = total[(k + 1) * quarter:(k + 2) * quarter].astype(bf16)

    return pl.pallas_call(
        body,
        grid=(cols // TILE,),
        in_specs=[
            pl.BlockSpec((tokens, half), lambda i: (0, 0), pipeline_mode=pl.Buffered(1)),
            pl.BlockSpec((tokens, TILE), lambda i: (0, start // TILE + i)),
            pl.BlockSpec((half, TILE), lambda i: (0, i)),
        ],
        out_specs=[pl.BlockSpec((quarter, TILE), lambda i: (0, i))] * 4,
        out_shape=[jax.ShapeDtypeStruct((quarter, cols), f32)] + [jax.ShapeDtypeStruct((quarter, cols), bf16)] * 3,
        name="chip_product",
        cost_estimate=cost(tokens, half, cols),
        compiler_params=params(),
    )(mine, out_grad, received)


def windows(lengths, pieces):
    cap = pieces[0].size
    n, rows = cap // 256, cap // 128

    def body(s, p0, p1, p2, out, held):
        group = s[N_GRP]
        begin = jnp.int32(0)
        for k in range(N_GRP):
            begin = begin + jnp.where(k < group, s[k], 0)
        length = s[group]
        lane = lax.broadcasted_iota(jnp.int32, (n, 128), 1)
        at = lax.broadcasted_iota(jnp.int32, (n, 128), 0) * 128 + lane
        for k, piece in enumerate((p0, p1, p2)):
            held[pl.ds(n, rows), :] = piece[...]
            for target in range(N_GRP):
                offset = target * n * 128 - begin
                first = jnp.clip(offset >> 7, -n, rows) + n
                turn = offset & 127
                back = (128 - turn) & 127
                low = pltpu.roll(held[pl.ds(first, n), :], back, 1)
                high = pltpu.roll(held[pl.ds(first + 1, n), :], back, 1)
                value = jnp.where(lane < 128 - turn, low, high)
                inside = (at + offset >= 0) & (at + offset < length)
                out[target, k] = jnp.where(inside, value, 0.0).astype(bf16)

    whole = pl.BlockSpec((rows, 128), lambda i, s: (0, 0))
    return pl.pallas_call(
        body,
        grid_spec=pltpu.PrefetchScalarGridSpec(
            num_scalar_prefetch=1,
            grid=(1,),
            in_specs=[whole] * 3,
            out_specs=pl.BlockSpec((N_GRP, 3, n, 128), lambda i, s: (0, 0, 0, 0)),
            scratch_shapes=[pltpu.VMEM((rows + 2 * n + 8, 128), f32)],
        ),
        out_shape=jax.ShapeDtypeStruct((N_GRP, 3, n, 128), bf16),
        name="windows",
        cost_estimate=pl.CostEstimate(flops=10**7, bytes_accessed=4 * 10**6, transcendentals=0),
        compiler_params=params(),
    )(lengths, *[a.reshape(rows, 128) for a in pieces])


def local(context, out_grad, old_master, old_mom1, old_mom2, old_lengths):
    width = out_grad.shape[1]
    table = row_table(lax.axis_index("shard"))
    scalars = jnp.concatenate([old_lengths[0], lax.axis_index("grp")[None]]).astype(jnp.int32)
    pieces = (old_master, old_mom1, old_mom2)

    first_cols, second_cols = CHUNKS
    theirs, mine, other = first_product(table, context, out_grad, 0, first_cols)
    received = lax.ppermute(theirs, AXES, SWAP)
    theirs = other_product(other, out_grad, first_cols, second_cols)
    received_later = lax.ppermute(theirs, AXES, SWAP)
    (received, mine), theirs = lax.optimization_barrier(((received, mine), theirs))
    own, *away = chip_product(mine, out_grad, received, 0, first_cols)
    (own, away), pieces, mine = lax.optimization_barrier(((own, away), pieces, mine))
    arrived = [lax.ppermute(away[k - 1], AXES, FIRST[k]) for k in (1, 2, 3)]
    cut = windows(scalars, pieces)
    cut, mine = lax.optimization_barrier((cut, mine))
    state = lax.all_to_all(cut, "grp", 0, 0, tiled=True)
    own_later, *away = chip_product(mine, out_grad, received_later, first_cols, second_cols)
    arrived, own_later = lax.optimization_barrier((arrived, own_later))
    arrived_later = [lax.ppermute(away[k - 1], AXES, FIRST[k]) for k in (1, 2, 3)]
    columns = [(0, first_cols, own, arrived), (first_cols, second_cols, own_later, arrived_later)]
    state = jnp.sum(state.astype(f32), axis=0).reshape(3, ROWS // N_GRP, width)

    results = []
    for start, cols, own, arrived in columns:
        summed = own
        for value in arrived:
            summed = summed + value.astype(f32)
        summed = summed.astype(bf16).reshape(16, ROWS // N_GRP, cols)
        summed = lax.all_to_all(summed, AXES, 0, 0, axis_index_groups=SECOND, tiled=True)
        gradient = jnp.sum(summed.astype(f32), axis=0)
        master, first, second = state[:, :, start:start + cols]
        first_new = beta_one * first + (1.0 - beta_one) * gradient
        second_new = beta_two * second + (1.0 - beta_two) * gradient * gradient
        master_new = master - step_size * first_new / (jnp.sqrt(second_new) + epsilon)
        results.append((master_new, first_new, second_new))
    master_new, first_new, second_new = [jnp.concatenate(parts, axis=1) for parts in zip(*results)]
    weights = jnp.broadcast_to(master_new.astype(bf16)[None], (N_GRP,) + master_new.shape)
    weights = lax.all_to_all(weights, "grp", 0, 0, tiled=True).reshape(ROWS, width)
    return (master_new[None], first_new[None], second_new[None], weights[None])


def solution(mesh):
    placed = (
        P(("grp", "shard"), None),
        P(("grp", "shard"), None),
        P("shard", "grp", None),
        P("shard", "grp", None),
        P("shard", "grp", None),
        P("shard", None),
    )
    return jax.shard_map(
        local,
        mesh=mesh,
        in_specs=placed,
        out_specs=(
            P("shard", "grp", None),
            P("shard", "grp", None),
            P("shard", "grp", None),
            P("shard", None, None),
        ),
        check_vma=False,
    )
```

```python
import jax
import jax.numpy as jnp
from jax import lax
from jax.experimental import pallas as pl
from jax.experimental.pallas import tpu as pltpu
from jax.sharding import PartitionSpec as P

beta_one = 0.9
beta_two = 0.95
step_size = 0.01
epsilon = 1e-08

N_GRP = 4
ROWS = 64
CHUNKS = (2048, 2048)
TILE = 512
f32, bf16 = jnp.float32, jnp.bfloat16
AXES = ("grp", "shard")

DEVICES = [(z, y, x, c) for z in range(4) for y in range(4) for x in range(4) for c in range(2)]
SWAP = [(i, i ^ 1) for i in range(128)]


def number(z, y, x, c):
    return (((z % 4) * 4 + y % 4) * 4 + x % 4) * 2 + c


FIRST = {
    k: [(number(z, y, x, c), number(z, y + k * c, x + k * (1 - c), c)) for z, y, x, c in DEVICES] for k in (1, 2, 3)
}


def grouped(key, order):
    groups = {}
    for place in sorted(DEVICES, key=lambda place: order(*place)):
        groups.setdefault(key(*place), []).append(number(*place))
    return list(groups.values())


THIRD = {k: [(number(z, y, x, c), number(z + k, y, x, c)) for z, y, x, c in DEVICES] for k in (1, 2, 3)}
ALONG_FIRST = grouped(lambda z, y, x, c: (z, c, x if c else y), lambda z, y, x, c: (y, x))
SECOND = grouped(lambda z, y, x, c: (c, y if c else x), lambda z, y, x, c: (y, x, z))


def row_block(shard, core, i):
    x, y, j1, d2 = (shard >> 1) & 3, shard >> 3, i // 4, i % 4
    return jnp.where(core == 0, d2 * 4 + ((x + j1) & 3), ((y + j1) & 3) * 4 + d2)


def params():
    return pltpu.CompilerParams(vmem_limit_bytes=60 * 2**20)


def cost(tokens, height, cols):
    return pl.CostEstimate(
        flops=2 * tokens * height * cols // 16, bytes_accessed=(tokens + height) * cols // 8, transcendentals=0
    )


def product(left, right):
    return lax.dot_general(left, right, (((0,), (0,)), ((), ())), preferred_element_type=f32)


def first_product(shard, context, out_grad, start, cols):
    tokens, height = context.shape
    half, parts = height // 2, 4
    slab = tokens // parts

    def body(t, c_hbm, g, out, mine_hbm, other_hbm, c, mine, other, arrived, left):
        step = pl.program_id(0)

        def piece(m):
            at = pl.ds(m * slab, slab)
            return pltpu.make_async_copy(c_hbm.at[at], c.at[at], arrived.at[m])

        def away():
            return [
                pltpu.make_async_copy(mine, mine_hbm, left.at[0]),
                pltpu.make_async_copy(other, other_hbm, left.at[1]),
            ]

        def choose(to, core):
            for m in range(parts):
                at = pl.ds(m * slab, slab)
                for k in range(8):
                    low, high = [
                        c[at, pl.ds(pl.multiple_of(row_block(t[0], core, 2 * k + i) * 128, 128), 128)] for i in (0, 1)
                    ]
                    to[at, pl.ds(k * 128, 128)] = jnp.concatenate(
                        [low[:, core * 64:core * 64 + 64], high[:, core * 64:core * 64 + 64]], axis=1
                    )

        @pl.when(step == 0)
        def _():
            for m in range(parts):
                piece(m).start()
            for m in range(parts):
                piece(m).wait()

            @pl.when((t[0] & 1) == 0)
            def _():
                choose(other, 1)
                choose(mine, 0)

            @pl.when((t[0] & 1) == 1)
            def _():
                choose(other, 0)
                choose(mine, 1)

            for copy in away():
                copy.start()

        out[...] = product(other[...], g[...]).astype(bf16)

        @pl.when(step == cols // TILE - 1)
        def _():
            for copy in away():
                copy.wait()

    hbm = pl.BlockSpec(memory_space=pl.ANY)
    return pl.pallas_call(
        body,
        grid_spec=pltpu.PrefetchScalarGridSpec(
            num_scalar_prefetch=1,
            grid=(cols // TILE,),
            in_specs=[hbm, pl.BlockSpec((tokens, TILE), lambda i, t: (0, start // TILE + i))],
            out_specs=[pl.BlockSpec((half, TILE), lambda i, t: (0, i)), hbm, hbm],
            scratch_shapes=[
                pltpu.VMEM((tokens, height), bf16),
                pltpu.VMEM((tokens, half), bf16),
                pltpu.VMEM((tokens, half), bf16),
                pltpu.SemaphoreType.DMA((parts,)),
                pltpu.SemaphoreType.DMA((2,)),
            ],
        ),
        out_shape=[
            jax.ShapeDtypeStruct((half, cols), bf16),
            jax.ShapeDtypeStruct((tokens, half), bf16),
            jax.ShapeDtypeStruct((tokens, half), bf16),
        ],
        name="first_product",
        cost_estimate=cost(tokens, half, cols),
        compiler_params=params(),
    )(shard, context, out_grad)


def other_product(other, out_grad, start, cols):
    tokens, half = other.shape

    def body(c, g, out):
        out[...] = product(c[...], g[...]).astype(bf16)

    return pl.pallas_call(
        body,
        grid=(cols // TILE,),
        in_specs=[
            pl.BlockSpec((tokens, half), lambda i: (0, 0), pipeline_mode=pl.Buffered(1)),
            pl.BlockSpec((tokens, TILE), lambda i: (0, start // TILE + i)),
        ],
        out_specs=pl.BlockSpec((half, TILE), lambda i: (0, i)),
        out_shape=jax.ShapeDtypeStruct((half, cols), bf16),
        name="other_product",
        cost_estimate=cost(tokens, half, cols),
        compiler_params=params(),
    )(other, out_grad)


def chip_product(shard, mine, out_grad, received, start, cols, by_place):
    tokens, half = mine.shape
    quarter = half // 4

    def body(t, c, g, r, own, *away):
        total = product(c[...], g[...]) + r[...].astype(f32)
        own[...] = total[:quarter]
        if by_place:
            place = jnp.where((t[0] & 1) == 0, (t[0] >> 1) & 3, t[0] >> 3)
            for k in range(4):
                away[0][(place + k) & 3] = total[k * quarter:(k + 1) * quarter].astype(bf16)
        else:
            for k in range(3):
                away[k][...] = total[(k + 1) * quarter:(k + 2) * quarter].astype(bf16)

    spec = pl.BlockSpec((quarter, TILE), lambda i, t: (0, i))
    if by_place:
        specs, shapes = [pl.BlockSpec((4, quarter, TILE), lambda i, t: (0, 0, i))], [(4, quarter, cols)]
    else:
        specs, shapes = [spec] * 3, [(quarter, cols)] * 3
    return pl.pallas_call(
        body,
        grid_spec=pltpu.PrefetchScalarGridSpec(
            num_scalar_prefetch=1,
            grid=(cols // TILE,),
            in_specs=[
                pl.BlockSpec((tokens, half), lambda i, t: (0, 0), pipeline_mode=pl.Buffered(1)),
                pl.BlockSpec((tokens, TILE), lambda i, t: (0, start // TILE + i)),
                pl.BlockSpec((half, TILE), lambda i, t: (0, i)),
            ],
            out_specs=[spec] + specs,
        ),
        out_shape=[jax.ShapeDtypeStruct((quarter, cols), f32)] + [jax.ShapeDtypeStruct(shape, bf16) for shape in shapes],
        name="chip_product",
        cost_estimate=cost(tokens, half, cols),
        compiler_params=params(),
    )(shard, mine, out_grad, received)


def windows(lengths, group, pieces):
    cap = pieces[0].size
    n, rows = cap // 256, cap // 128

    def body(s, g, p0, p1, p2, *refs):
        group, held = g[0], refs[N_GRP]
        begin = jnp.int32(0)
        for k in range(N_GRP):
            begin = begin + jnp.where(k < group, s[k], 0)
        length = s[group]
        lane = lax.broadcasted_iota(jnp.int32, (n, 128), 1)
        at = lax.broadcasted_iota(jnp.int32, (n, 128), 0) * 128 + lane
        for k, piece in enumerate((p0, p1, p2)):
            held[pl.ds(n, rows), :] = piece[...]
            for further in range(N_GRP):
                offset = ((group + further) & (N_GRP - 1)) * (n * 128) - begin
                first = jnp.clip(offset >> 7, -n, rows) + n
                turn = offset & 127
                back = (128 - turn) & 127
                low = pltpu.roll(held[pl.ds(first, n), :], back, 1)
                high = pltpu.roll(held[pl.ds(first + 1, n), :], back, 1)
                value = jnp.where(lane < 128 - turn, low, high)
                inside = (at + offset >= 0) & (at + offset < length)
                refs[further][k] = jnp.where(inside, value, 0.0).astype(bf16)

    whole = pl.BlockSpec((rows, 128), lambda i, s, g: (0, 0))
    return pl.pallas_call(
        body,
        grid_spec=pltpu.PrefetchScalarGridSpec(
            num_scalar_prefetch=2,
            grid=(1,),
            in_specs=[whole] * 3,
            out_specs=[pl.BlockSpec((3, n, 128), lambda i, s, g: (0, 0, 0))] * N_GRP,
            scratch_shapes=[pltpu.VMEM((rows + 2 * n + 8, 128), f32)],
        ),
        out_shape=[jax.ShapeDtypeStruct((3, n, 128), bf16)] * N_GRP,
        name="windows",
        cost_estimate=pl.CostEstimate(flops=10**7, bytes_accessed=4 * 10**6, transcendentals=0),
        compiler_params=params(),
    )(lengths, group, *[a.reshape(rows, 128) for a in pieces])


def local(context, out_grad, old_master, old_mom1, old_mom2, old_lengths):
    width = out_grad.shape[1]
    shard, group = lax.axis_index("shard")[None], lax.axis_index("grp")[None]
    first_cols, second_cols = CHUNKS

    theirs, mine, other = first_product(shard, context, out_grad, 0, first_cols)
    received = lax.ppermute(theirs, AXES, SWAP)
    theirs = other_product(other, out_grad, first_cols, second_cols)
    received_later = lax.ppermute(theirs, AXES, SWAP)
    (received, mine), theirs = lax.optimization_barrier(((received, mine), theirs))
    own, away = chip_product(shard, mine, out_grad, received, 0, first_cols, True)
    (own, away), mine = lax.optimization_barrier(((own, away), mine))
    arrived = lax.all_to_all(away, AXES, 0, 0, axis_index_groups=ALONG_FIRST, tiled=True)
    own_later, *away = chip_product(shard, mine, out_grad, received_later, first_cols, second_cols, False)
    pieces = (old_master, old_mom1, old_mom2)
    pieces, own_later = lax.optimization_barrier((pieces, own_later))
    arrived_later = [lax.ppermute(away[k - 1], AXES, FIRST[k]) for k in (1, 2, 3)]
    keep, *cut = windows(old_lengths[0], group, pieces)
    (keep, cut), own = lax.optimization_barrier(((keep, cut), own))
    cut = [lax.ppermute(cut[k - 1], AXES, THIRD[k]) for k in (1, 2, 3)]
    state = sum([value.astype(f32) for value in cut], keep.astype(f32)).reshape(3, ROWS // N_GRP, width)

    def first_sum(own, arrived):
        return sum([value.astype(f32) for value in arrived], own).astype(bf16)

    def owners(summed):
        summed = summed.reshape(16, ROWS // N_GRP, -1)
        return lax.all_to_all(summed, AXES, 0, 0, axis_index_groups=SECOND, tiled=True)

    def step(state, gradient):
        gradient = jnp.sum(gradient.astype(f32), axis=0)
        master, first, second = state
        first_new = beta_one * first + (1.0 - beta_one) * gradient
        second_new = beta_two * second + (1.0 - beta_two) * gradient * gradient
        return master - step_size * first_new / (jnp.sqrt(second_new) + epsilon), first_new, second_new

    place = jnp.where(shard[0] % 2 == 0, shard[0] // 2 % 4, shard[0] // 8)
    summed = first_sum(own, [jnp.where(place == k, 0.0, arrived[k].astype(f32)) for k in range(4)])
    summed, own_later = lax.optimization_barrier((summed, own_later))
    own_later, state = lax.optimization_barrier((own_later, state))
    terms = owners(summed)
    summed_later = first_sum(own_later, arrived_later)
    summed_later, terms = lax.optimization_barrier((summed_later, terms))
    terms_later = owners(summed_later)
    def to_groups(part):
        parts = [part] + [lax.ppermute(part, AXES, THIRD[k]) for k in (1, 2, 3)]
        whole = jnp.zeros((N_GRP,) + part.shape, bf16)
        for k, part in enumerate(parts):
            whole = lax.dynamic_update_index_in_dim(whole, part, (group[0] - k) % N_GRP, 0)
        return whole.reshape(ROWS, -1)

    result = step(state[:, :, :first_cols], terms)
    weights = to_groups(result[0].astype(bf16))
    weights, terms_later = lax.optimization_barrier((weights, terms_later))
    result_later = step(state[:, :, first_cols:], terms_later)
    weights = [weights, to_groups(result_later[0].astype(bf16))]
    outputs = [*zip(result, result_later), weights]
    return tuple(jnp.concatenate(parts, axis=1)[None] for parts in outputs)


def solution(mesh):
    placed = (
        P(("grp", "shard"), None),
        P(("grp", "shard"), None),
        P("shard", "grp", None),
        P("shard", "grp", None),
        P("shard", "grp", None),
        P("shard", None),
    )
    return jax.shard_map(
        local,
        mesh=mesh,
        in_specs=placed,
        out_specs=(
            P("shard", "grp", None),
            P("shard", "grp", None),
            P("shard", "grp", None),
            P("shard", None, None),
        ),
        check_vma=False,
    )
```

```python
import jax
import jax.numpy as jnp
from jax import lax
from jax.experimental import pallas as pl
from jax.experimental.pallas import tpu as pltpu
from jax.sharding import PartitionSpec as P

beta_one = 0.9
beta_two = 0.95
step_size = 0.01
epsilon = 1e-08

N_GRP = 4
ROWS = 64
CHUNKS = (2048, 2048)
TILE = 512
f32, bf16 = jnp.float32, jnp.bfloat16
AXES = ("grp", "shard")

DEVICES = [(z, y, x, c) for z in range(4) for y in range(4) for x in range(4) for c in range(2)]
SWAP = [(i, i ^ 1) for i in range(128)]


def number(z, y, x, c):
    return (((z % 4) * 4 + y % 4) * 4 + x % 4) * 2 + c


FIRST = {
    k: [(number(z, y, x, c), number(z, y + k * c, x + k * (1 - c), c)) for z, y, x, c in DEVICES] for k in (1, 2, 3)
}


def grouped(key, order):
    groups = {}
    for place in sorted(DEVICES, key=lambda place: order(*place)):
        groups.setdefault(key(*place), []).append(number(*place))
    return list(groups.values())


THIRD = {k: [(number(z, y, x, c), number(z + k, y, x, c)) for z, y, x, c in DEVICES] for k in (1, 2, 3)}
ALONG_FIRST = grouped(lambda z, y, x, c: (z, c, x if c else y), lambda z, y, x, c: (y, x))
SECOND = grouped(lambda z, y, x, c: (c, y if c else x), lambda z, y, x, c: (y, x, z))


def row_block(shard, core, i):
    x, y, j1, d2 = (shard >> 1) & 3, shard >> 3, i // 4, i % 4
    return jnp.where(core == 0, d2 * 4 + ((x + j1) & 3), ((y + j1) & 3) * 4 + d2)


def params():
    return pltpu.CompilerParams(vmem_limit_bytes=60 * 2**20)


def cost(tokens, height, cols):
    return pl.CostEstimate(
        flops=2 * tokens * height * cols // 16, bytes_accessed=(tokens + height) * cols // 8, transcendentals=0
    )


def product(left, right):
    return lax.dot_general(left, right, (((0,), (0,)), ((), ())), preferred_element_type=f32)


def first_product(shard, context, out_grad, start, cols):
    tokens, height = context.shape
    half, parts = height // 2, 4
    slab = tokens // parts

    def body(t, c_hbm, g, out, mine_hbm, other_hbm, c, mine, other, arrived, left):
        step = pl.program_id(0)

        def piece(m):
            at = pl.ds(m * slab, slab)
            return pltpu.make_async_copy(c_hbm.at[at], c.at[at], arrived.at[m])

        def away():
            return [
                pltpu.make_async_copy(mine, mine_hbm, left.at[0]),
                pltpu.make_async_copy(other, other_hbm, left.at[1]),
            ]

        def choose(to, core, at):
            for k in range(8):
                low, high = [
                    c[at, pl.ds(pl.multiple_of(row_block(t[0], core, 2 * k + i) * 128, 128), 128)] for i in (0, 1)
                ]
                to[at, pl.ds(k * 128, 128)] = jnp.concatenate(
                    [low[:, core * 64:core * 64 + 64], high[:, core * 64:core * 64 + 64]], axis=1
                )

        def choose_all(core):
            for m in range(parts):
                piece(m).wait()
                choose(other, 1 - core, pl.ds(m * slab, slab))
                choose(mine, core, pl.ds(m * slab, slab))

        @pl.when(step == 0)
        def _():
            for m in range(parts):
                piece(m).start()

            @pl.when((t[0] & 1) == 0)
            def _():
                choose_all(0)

            @pl.when((t[0] & 1) == 1)
            def _():
                choose_all(1)

            for copy in away():
                copy.start()

        out[...] = product(other[...], g[...]).astype(bf16)

        @pl.when(step == cols // TILE - 1)
        def _():
            for copy in away():
                copy.wait()

    hbm = pl.BlockSpec(memory_space=pl.ANY)
    return pl.pallas_call(
        body,
        grid_spec=pltpu.PrefetchScalarGridSpec(
            num_scalar_prefetch=1,
            grid=(cols // TILE,),
            in_specs=[hbm, pl.BlockSpec((tokens, TILE), lambda i, t: (0, start // TILE + i))],
            out_specs=[pl.BlockSpec((half, TILE), lambda i, t: (0, i)), hbm, hbm],
            scratch_shapes=[
                pltpu.VMEM((tokens, height), bf16),
                pltpu.VMEM((tokens, half), bf16),
                pltpu.VMEM((tokens, half), bf16),
                pltpu.SemaphoreType.DMA((parts,)),
                pltpu.SemaphoreType.DMA((2,)),
            ],
        ),
        out_shape=[
            jax.ShapeDtypeStruct((half, cols), bf16),
            jax.ShapeDtypeStruct((tokens, half), bf16),
            jax.ShapeDtypeStruct((tokens, half), bf16),
        ],
        name="first_product",
        cost_estimate=cost(tokens, half, cols),
        compiler_params=params(),
    )(shard, context, out_grad)


def other_product(other, out_grad, start, cols):
    tokens, half = other.shape

    def body(c, g, out):
        out[...] = product(c[...], g[...]).astype(bf16)

    return pl.pallas_call(
        body,
        grid=(cols // TILE,),
        in_specs=[
            pl.BlockSpec((tokens, half), lambda i: (0, 0), pipeline_mode=pl.Buffered(1)),
            pl.BlockSpec((tokens, TILE), lambda i: (0, start // TILE + i)),
        ],
        out_specs=pl.BlockSpec((half, TILE), lambda i: (0, i)),
        out_shape=jax.ShapeDtypeStruct((half, cols), bf16),
        name="other_product",
        cost_estimate=cost(tokens, half, cols),
        compiler_params=params(),
    )(other, out_grad)


def chip_product(shard, mine, out_grad, received, start, cols, by_place):
    tokens, half = mine.shape
    quarter = half // 4

    def body(t, c, g, r, own, *away):
        total = product(c[...], g[...]) + r[...].astype(f32)
        own[...] = total[:quarter]
        if by_place:
            place = jnp.where((t[0] & 1) == 0, (t[0] >> 1) & 3, t[0] >> 3)
            for k in range(4):
                away[0][(place + k) & 3] = total[k * quarter:(k + 1) * quarter].astype(bf16)
        else:
            for k in range(3):
                away[k][...] = total[(k + 1) * quarter:(k + 2) * quarter].astype(bf16)

    spec = pl.BlockSpec((quarter, TILE), lambda i, t: (0, i))
    if by_place:
        specs, shapes = [pl.BlockSpec((4, quarter, TILE), lambda i, t: (0, 0, i))], [(4, quarter, cols)]
    else:
        specs, shapes = [spec] * 3, [(quarter, cols)] * 3
    return pl.pallas_call(
        body,
        grid_spec=pltpu.PrefetchScalarGridSpec(
            num_scalar_prefetch=1,
            grid=(cols // TILE,),
            in_specs=[
                pl.BlockSpec((tokens, half), lambda i, t: (0, 0), pipeline_mode=pl.Buffered(1)),
                pl.BlockSpec((tokens, TILE), lambda i, t: (0, start // TILE + i)),
                pl.BlockSpec((half, TILE), lambda i, t: (0, i)),
            ],
            out_specs=[spec] + specs,
        ),
        out_shape=[jax.ShapeDtypeStruct((quarter, cols), f32)] + [jax.ShapeDtypeStruct(shape, bf16) for shape in shapes],
        name="chip_product",
        cost_estimate=cost(tokens, half, cols),
        compiler_params=params(),
    )(shard, mine, out_grad, received)


def windows(lengths, group, pieces):
    cap = pieces[0].size
    n, rows = cap // 256, cap // 128

    def body(s, g, p0, p1, p2, *refs):
        group, held = g[0], refs[N_GRP]
        begin = jnp.int32(0)
        for k in range(N_GRP):
            begin = begin + jnp.where(k < group, s[k], 0)
        length = s[group]
        lane = lax.broadcasted_iota(jnp.int32, (n, 128), 1)
        at = lax.broadcasted_iota(jnp.int32, (n, 128), 0) * 128 + lane
        for k, piece in enumerate((p0, p1, p2)):
            held[pl.ds(n, rows), :] = piece[...]
            for further in range(N_GRP):
                offset = ((group + further) & (N_GRP - 1)) * (n * 128) - begin
                first = jnp.clip(offset >> 7, -n, rows) + n
                turn = offset & 127
                back = (128 - turn) & 127
                low = pltpu.roll(held[pl.ds(first, n), :], back, 1)
                high = pltpu.roll(held[pl.ds(first + 1, n), :], back, 1)
                value = jnp.where(lane < 128 - turn, low, high)
                inside = (at + offset >= 0) & (at + offset < length)
                refs[further][k] = jnp.where(inside, value, 0.0).astype(bf16)

    whole = pl.BlockSpec((rows, 128), lambda i, s, g: (0, 0))
    return pl.pallas_call(
        body,
        grid_spec=pltpu.PrefetchScalarGridSpec(
            num_scalar_prefetch=2,
            grid=(1,),
            in_specs=[whole] * 3,
            out_specs=[pl.BlockSpec((3, n, 128), lambda i, s, g: (0, 0, 0))] * N_GRP,
            scratch_shapes=[pltpu.VMEM((rows + 2 * n + 8, 128), f32)],
        ),
        out_shape=[jax.ShapeDtypeStruct((3, n, 128), bf16)] * N_GRP,
        name="windows",
        cost_estimate=pl.CostEstimate(flops=10**7, bytes_accessed=4 * 10**6, transcendentals=0),
        compiler_params=params(),
    )(lengths, group, *[a.reshape(rows, 128) for a in pieces])


def local(context, out_grad, old_master, old_mom1, old_mom2, old_lengths):
    width = out_grad.shape[1]
    shard, group = lax.axis_index("shard")[None], lax.axis_index("grp")[None]
    first_cols, second_cols = CHUNKS

    theirs, mine, other = first_product(shard, context, out_grad, 0, first_cols)
    received = lax.ppermute(theirs, AXES, SWAP)
    theirs = other_product(other, out_grad, first_cols, second_cols)
    received_later = lax.ppermute(theirs, AXES, SWAP)
    (received, mine), theirs = lax.optimization_barrier(((received, mine), theirs))
    own, away = chip_product(shard, mine, out_grad, received, 0, first_cols, True)
    pieces = (old_master, old_mom1, old_mom2)
    (own, away), pieces = lax.optimization_barrier(((own, away), pieces))
    arrived = lax.all_to_all(away, AXES, 0, 0, axis_index_groups=ALONG_FIRST, tiled=True)
    keep, *cut = windows(old_lengths[0], group, pieces)
    (keep, cut), mine = lax.optimization_barrier(((keep, cut), mine))
    cut = [lax.ppermute(cut[k - 1], AXES, THIRD[k]) for k in (1, 2, 3)]
    own_later, *away = chip_product(shard, mine, out_grad, received_later, first_cols, second_cols, False)
    cut, arrived, own_later = lax.optimization_barrier((cut, arrived, own_later))
    arrived_later = [lax.ppermute(away[k - 1], AXES, FIRST[k]) for k in (1, 2, 3)]
    state = sum([value.astype(f32) for value in cut], keep.astype(f32)).reshape(3, ROWS // N_GRP, width)

    def first_sum(own, arrived):
        return sum([value.astype(f32) for value in arrived], own).astype(bf16)

    def owners(summed):
        summed = summed.reshape(16, ROWS // N_GRP, -1)
        return lax.all_to_all(summed, AXES, 0, 0, axis_index_groups=SECOND, tiled=True)

    def step(state, gradient):
        gradient = jnp.sum(gradient.astype(f32), axis=0)
        master, first, second = state
        first_new = beta_one * first + (1.0 - beta_one) * gradient
        second_new = beta_two * second + (1.0 - beta_two) * gradient * gradient
        return master - step_size * first_new / (jnp.sqrt(second_new) + epsilon), first_new, second_new

    place = jnp.where(shard[0] % 2 == 0, shard[0] // 2 % 4, shard[0] // 8)
    summed = first_sum(own, [jnp.where(place == k, 0.0, arrived[k].astype(f32)) for k in range(4)])
    summed, own_later = lax.optimization_barrier((summed, own_later))
    terms = owners(summed)
    summed_later = first_sum(own_later, arrived_later)
    summed_later, terms = lax.optimization_barrier((summed_later, terms))
    terms_later = owners(summed_later)
    def to_groups(part):
        parts = [part] + [lax.ppermute(part, AXES, THIRD[k]) for k in (1, 2, 3)]
        whole = jnp.zeros((N_GRP,) + part.shape, bf16)
        for k, part in enumerate(parts):
            whole = lax.dynamic_update_index_in_dim(whole, part, (group[0] - k) % N_GRP, 0)
        return whole.reshape(ROWS, -1)

    results = [step(state[:, :, :first_cols], terms), step(state[:, :, first_cols:], terms_later)]
    master_new, first_new, second_new = [jnp.concatenate(parts, axis=1) for parts in zip(*results)]
    weights = to_groups(master_new.astype(bf16))
    return (master_new[None], first_new[None], second_new[None], weights[None])


def solution(mesh):
    placed = (
        P(("grp", "shard"), None),
        P(("grp", "shard"), None),
        P("shard", "grp", None),
        P("shard", "grp", None),
        P("shard", "grp", None),
        P("shard", None),
    )
    return jax.shard_map(
        local,
        mesh=mesh,
        in_specs=placed,
        out_specs=(
            P("shard", "grp", None),
            P("shard", "grp", None),
            P("shard", "grp", None),
            P("shard", None, None),
        ),
        check_vma=False,
    )
```

```python
import jax
import jax.numpy as jnp
from jax import lax
from jax.experimental import pallas as pl
from jax.experimental.pallas import tpu as pltpu
from jax.sharding import PartitionSpec as P

beta_one = 0.9
beta_two = 0.95
step_size = 0.01
epsilon = 1e-08

N_GRP = 4
ROWS = 64
CHUNKS = (2048, 2048)
TILE = 512
f32, bf16 = jnp.float32, jnp.bfloat16
AXES = ("grp", "shard")

DEVICES = [(z, y, x, c) for z in range(4) for y in range(4) for x in range(4) for c in range(2)]
SWAP = [(i, i ^ 1) for i in range(128)]


def number(z, y, x, c):
    return (((z % 4) * 4 + y % 4) * 4 + x % 4) * 2 + c


FIRST = {
    k: [(number(z, y, x, c), number(z, y + k * c, x + k * (1 - c), c)) for z, y, x, c in DEVICES] for k in (1, 2, 3)
}


def grouped(key, order):
    groups = {}
    for place in sorted(DEVICES, key=lambda place: order(*place)):
        groups.setdefault(key(*place), []).append(number(*place))
    return list(groups.values())


THIRD = {k: [(number(z, y, x, c), number(z + k, y, x, c)) for z, y, x, c in DEVICES] for k in (1, 2, 3)}
ALONG_FIRST = grouped(lambda z, y, x, c: (z, c, x if c else y), lambda z, y, x, c: (y, x))
SECOND = grouped(lambda z, y, x, c: (c, y if c else x), lambda z, y, x, c: (y, x, z))


def row_block(shard, core, i):
    x, y, j1, d2 = (shard >> 1) & 3, shard >> 3, i // 4, i % 4
    return jnp.where(core == 0, d2 * 4 + ((x + j1) & 3), ((y + j1) & 3) * 4 + d2)


def params():
    return pltpu.CompilerParams(vmem_limit_bytes=60 * 2**20)


def cost(tokens, height, cols):
    return pl.CostEstimate(
        flops=2 * tokens * height * cols // 16, bytes_accessed=(tokens + height) * cols // 8, transcendentals=0
    )


def product(left, right):
    return lax.dot_general(left, right, (((0,), (0,)), ((), ())), preferred_element_type=f32)


def first_product(shard, context, out_grad, start, cols):
    tokens, height = context.shape
    half, parts = height // 2, 8
    slab = tokens // parts

    def body(t, c_hbm, g, out, mine_hbm, other_hbm, c, mine, other, arrived, left):
        step = pl.program_id(0)

        def piece(m):
            at = pl.ds(m * slab, slab)
            return pltpu.make_async_copy(c_hbm.at[at], c.at[at], arrived.at[m])

        def away():
            return [
                pltpu.make_async_copy(mine, mine_hbm, left.at[0]),
                pltpu.make_async_copy(other, other_hbm, left.at[1]),
            ]

        def choose(to, core, at):
            for k in range(8):
                low, high = [
                    c[at, pl.ds(pl.multiple_of(row_block(t[0], core, 2 * k + i) * 128, 128), 128)] for i in (0, 1)
                ]
                to[at, pl.ds(k * 128, 128)] = jnp.concatenate(
                    [low[:, core * 64:core * 64 + 64], high[:, core * 64:core * 64 + 64]], axis=1
                )

        def choose_all(core):
            for m in range(parts):
                piece(m).wait()
                choose(other, 1 - core, pl.ds(m * slab, slab))
                choose(mine, core, pl.ds(m * slab, slab))

        @pl.when(step == 0)
        def _():
            for m in range(parts):
                piece(m).start()

            @pl.when((t[0] & 1) == 0)
            def _():
                choose_all(0)

            @pl.when((t[0] & 1) == 1)
            def _():
                choose_all(1)

            for copy in away():
                copy.start()

        out[...] = product(other[...], g[...]).astype(bf16)

        @pl.when(step == cols // TILE - 1)
        def _():
            for copy in away():
                copy.wait()

    hbm = pl.BlockSpec(memory_space=pl.ANY)
    return pl.pallas_call(
        body,
        grid_spec=pltpu.PrefetchScalarGridSpec(
            num_scalar_prefetch=1,
            grid=(cols // TILE,),
            in_specs=[hbm, pl.BlockSpec((tokens, TILE), lambda i, t: (0, start // TILE + i))],
            out_specs=[pl.BlockSpec((half, TILE), lambda i, t: (0, i)), hbm, hbm],
            scratch_shapes=[
                pltpu.VMEM((tokens, height), bf16),
                pltpu.VMEM((tokens, half), bf16),
                pltpu.VMEM((tokens, half), bf16),
                pltpu.SemaphoreType.DMA((parts,)),
                pltpu.SemaphoreType.DMA((2,)),
            ],
        ),
        out_shape=[
            jax.ShapeDtypeStruct((half, cols), bf16),
            jax.ShapeDtypeStruct((tokens, half), bf16),
            jax.ShapeDtypeStruct((tokens, half), bf16),
        ],
        name="first_product",
        cost_estimate=cost(tokens, half, cols),
        compiler_params=params(),
    )(shard, context, out_grad)


def other_product(other, out_grad, start, cols):
    tokens, half = other.shape

    def body(c, g, out):
        out[...] = product(c[...], g[...]).astype(bf16)

    return pl.pallas_call(
        body,
        grid=(cols // TILE,),
        in_specs=[
            pl.BlockSpec((tokens, half), lambda i: (0, 0), pipeline_mode=pl.Buffered(1)),
            pl.BlockSpec((tokens, TILE), lambda i: (0, start // TILE + i)),
        ],
        out_specs=pl.BlockSpec((half, TILE), lambda i: (0, i)),
        out_shape=jax.ShapeDtypeStruct((half, cols), bf16),
        name="other_product",
        cost_estimate=cost(tokens, half, cols),
        compiler_params=params(),
    )(other, out_grad)


def chip_product(shard, mine, out_grad, received, start, cols, by_place):
    tokens, half = mine.shape
    quarter = half // 4

    def body(t, c, g, r, own, *away):
        total = product(c[...], g[...]) + r[...].astype(f32)
        own[...] = total[:quarter]
        if by_place:
            place = jnp.where((t[0] & 1) == 0, (t[0] >> 1) & 3, t[0] >> 3)
            for k in range(4):
                away[0][(place + k) & 3] = total[k * quarter:(k + 1) * quarter].astype(bf16)
        else:
            for k in range(3):
                away[k][...] = total[(k + 1) * quarter:(k + 2) * quarter].astype(bf16)

    spec = pl.BlockSpec((quarter, TILE), lambda i, t: (0, i))
    if by_place:
        specs, shapes = [pl.BlockSpec((4, quarter, TILE), lambda i, t: (0, 0, i))], [(4, quarter, cols)]
    else:
        specs, shapes = [spec] * 3, [(quarter, cols)] * 3
    return pl.pallas_call(
        body,
        grid_spec=pltpu.PrefetchScalarGridSpec(
            num_scalar_prefetch=1,
            grid=(cols // TILE,),
            in_specs=[
                pl.BlockSpec((tokens, half), lambda i, t: (0, 0), pipeline_mode=pl.Buffered(1)),
                pl.BlockSpec((tokens, TILE), lambda i, t: (0, start // TILE + i)),
                pl.BlockSpec((half, TILE), lambda i, t: (0, i)),
            ],
            out_specs=[spec] + specs,
        ),
        out_shape=[jax.ShapeDtypeStruct((quarter, cols), f32)] + [jax.ShapeDtypeStruct(shape, bf16) for shape in shapes],
        name="chip_product",
        cost_estimate=cost(tokens, half, cols),
        compiler_params=params(),
    )(shard, mine, out_grad, received)


def windows(lengths, group, pieces):
    cap = pieces[0].size
    n, rows = cap // 256, cap // 128

    def body(s, g, p0, p1, p2, *refs):
        group, held = g[0], refs[N_GRP]
        begin = jnp.int32(0)
        for k in range(N_GRP):
            begin = begin + jnp.where(k < group, s[k], 0)
        length = s[group]
        lane = lax.broadcasted_iota(jnp.int32, (n, 128), 1)
        at = lax.broadcasted_iota(jnp.int32, (n, 128), 0) * 128 + lane
        for k, piece in enumerate((p0, p1, p2)):
            held[pl.ds(n, rows), :] = piece[...]
            for further in range(N_GRP):
                offset = ((group + further) & (N_GRP - 1)) * (n * 128) - begin
                first = jnp.clip(offset >> 7, -n, rows) + n
                turn = offset & 127
                back = (128 - turn) & 127
                low = pltpu.roll(held[pl.ds(first, n), :], back, 1)
                high = pltpu.roll(held[pl.ds(first + 1, n), :], back, 1)
                value = jnp.where(lane < 128 - turn, low, high)
                inside = (at + offset >= 0) & (at + offset < length)
                refs[further][k] = jnp.where(inside, value, 0.0).astype(bf16)

    whole = pl.BlockSpec((rows, 128), lambda i, s, g: (0, 0))
    return pl.pallas_call(
        body,
        grid_spec=pltpu.PrefetchScalarGridSpec(
            num_scalar_prefetch=2,
            grid=(1,),
            in_specs=[whole] * 3,
            out_specs=[pl.BlockSpec((3, n, 128), lambda i, s, g: (0, 0, 0))] * N_GRP,
            scratch_shapes=[pltpu.VMEM((rows + 2 * n + 8, 128), f32)],
        ),
        out_shape=[jax.ShapeDtypeStruct((3, n, 128), bf16)] * N_GRP,
        name="windows",
        cost_estimate=pl.CostEstimate(flops=10**7, bytes_accessed=4 * 10**6, transcendentals=0),
        compiler_params=params(),
    )(lengths, group, *[a.reshape(rows, 128) for a in pieces])


def local(context, out_grad, old_master, old_mom1, old_mom2, old_lengths):
    width = out_grad.shape[1]
    shard, group = lax.axis_index("shard")[None], lax.axis_index("grp")[None]
    first_cols, second_cols = CHUNKS

    theirs, mine, other = first_product(shard, context, out_grad, 0, first_cols)
    received = lax.ppermute(theirs, AXES, SWAP)
    theirs = other_product(other, out_grad, first_cols, second_cols)
    received_later = lax.ppermute(theirs, AXES, SWAP)
    (received, mine), theirs = lax.optimization_barrier(((received, mine), theirs))
    own, away = chip_product(shard, mine, out_grad, received, 0, first_cols, True)
    pieces = (old_master, old_mom1, old_mom2)
    (own, away), pieces = lax.optimization_barrier(((own, away), pieces))
    arrived = lax.all_to_all(away, AXES, 0, 0, axis_index_groups=ALONG_FIRST, tiled=True)
    keep, *cut = windows(old_lengths[0], group, pieces)
    (keep, cut), mine = lax.optimization_barrier(((keep, cut), mine))
    own_later, *away = chip_product(shard, mine, out_grad, received_later, first_cols, second_cols, False)
    own_later, cut = lax.optimization_barrier((own_later, cut))
    arrived_later = [lax.ppermute(away[k - 1], AXES, FIRST[k]) for k in (1, 2, 3)]
    cut = [lax.ppermute(cut[k - 1], AXES, THIRD[k]) for k in (1, 2, 3)]
    cut[0], cut[2], arrived, own_later = lax.optimization_barrier((cut[0], cut[2], arrived, own_later))

    def first_sum(own, arrived):
        return sum([value.astype(f32) for value in arrived], own).astype(bf16)

    def owners(summed):
        summed = summed.reshape(16, ROWS // N_GRP, -1)
        return lax.all_to_all(summed, AXES, 0, 0, axis_index_groups=SECOND, tiled=True)

    def step(state, gradient):
        gradient = jnp.sum(gradient.astype(f32), axis=0)
        master, first, second = state
        first_new = beta_one * first + (1.0 - beta_one) * gradient
        second_new = beta_two * second + (1.0 - beta_two) * gradient * gradient
        return master - step_size * first_new / (jnp.sqrt(second_new) + epsilon), first_new, second_new

    place = jnp.where(shard[0] % 2 == 0, shard[0] // 2 % 4, shard[0] // 8)
    summed = first_sum(own, [lax.dynamic_index_in_dim(arrived, (place + k) % 4, 0, False) for k in (1, 2, 3)])
    summed, own_later, cut[1] = lax.optimization_barrier((summed, own_later, cut[1]))
    terms = owners(summed)
    state = sum([value.astype(f32) for value in cut], keep.astype(f32)).reshape(3, ROWS // N_GRP, width)
    summed_later = first_sum(own_later, arrived_later)
    summed_later, terms = lax.optimization_barrier((summed_later, terms))
    terms_later = owners(summed_later)
    def to_groups(part):
        parts = [part] + [lax.ppermute(part, AXES, THIRD[k]) for k in (1, 2, 3)]
        whole = jnp.zeros((N_GRP,) + part.shape, bf16)
        for k, part in enumerate(parts):
            whole = lax.dynamic_update_index_in_dim(whole, part, (group[0] - k) % N_GRP, 0)
        return whole.reshape(ROWS, -1)

    results = [step(state[:, :, :first_cols], terms), step(state[:, :, first_cols:], terms_later)]
    master_new, first_new, second_new = [jnp.concatenate(parts, axis=1) for parts in zip(*results)]
    weights = to_groups(master_new.astype(bf16))
    return (master_new[None], first_new[None], second_new[None], weights[None])


def solution(mesh):
    placed = (
        P(("grp", "shard"), None),
        P(("grp", "shard"), None),
        P("shard", "grp", None),
        P("shard", "grp", None),
        P("shard", "grp", None),
        P("shard", None),
    )
    return jax.shard_map(
        local,
        mesh=mesh,
        in_specs=placed,
        out_specs=(
            P("shard", "grp", None),
            P("shard", "grp", None),
            P("shard", "grp", None),
            P("shard", None, None),
        ),
        check_vma=False,
    )
```
